256 devices in a mesh: layer: 8 (over z_lo, x), dp: 32 (over z_hi, y, core).
Axes of the slice: x: 4, y: 4, z: 8 (z_hi: 4, z_lo: 2; z = z_hi * 2 + z_lo), core: 2. Of those that a mesh axis runs over, the one named last changes fastest.
Arguments:
- layer_inputs: bfloat16 [8, 8192, 5120], P('layer', 'dp'), may hold values from -6 to 6
- output_grads: bfloat16 [8, 8192, 13824], P('layer', 'dp'), may hold values from -6 to 6
- left_factors: bfloat16 [8, 32, 16, 13824], P('layer', 'dp'), may hold values from -0.0546875 to 0.0546875
- right_factors: bfloat16 [8, 32, 16, 5120], P('layer', 'dp'), may hold values from -0.078125 to 0.078125
- strengths: bfloat16 [8, 32, 16], P('layer', 'dp'), may hold values from 0.25 to 4
- train_ids: int32 [8192], P('dp'), may hold values from 0 to 100351
- query_ids: int32 [32, 64], replicated, may hold values from 0 to 100351
Outputs:
- token_scores: float32 [32, 8192], P('layer', 'dp')
- intersection: float32 [32, 4], P('layer')
The draws below stay inside these ranges and needn't reach their ends.
All inputs are finite; a program needn't handle non-finite values.
Results may differ from the reference program's by a relative error of at most 0.0003.
Values may be sent and summed in bfloat16 or wider, within the bound.
No kernel may reach another device: no remote copies, remote signals or barrier semaphores. Data moves between devices by JAX's collectives and lax.ppermute only.
A program may use at most 128 MiB of HBM per device.

```python
import math
import jax
import jax.numpy as jnp
import numpy as np
from jax import lax

D = 5120
FF = 13824
RANK = 16
QLEN = 64
VOCAB = 100352
SEQ_LEN = 2048
LAYERS = 8
TOKENS = 8192
QUERIES = 32


def place_ends(entries, stream_key, smallest, largest):
    index_at = [jax.random.randint(jax.random.fold_in(stream_key, axis), (), 0, length) for axis, length in enumerate(entries.shape)]
    main_axis = entries.shape.index(max(entries.shape))
    next_to = index_at[:main_axis] + [(index_at[main_axis] + 1) % entries.shape[main_axis]] + index_at[main_axis + 1:]
    return entries.at[tuple(index_at)].set(smallest).at[tuple(next_to)].set(largest)


def block_scale(rng, dims, shards, least, top_value):
    gain = 1.0
    for position, blocks in shards:
        draws = jax.random.uniform(jax.random.fold_in(jax.random.fold_in(rng, 6), position), (blocks,), jnp.float32, least / len(shards), top_value / len(shards))
        gain = gain * jnp.repeat(jnp.exp(draws), dims[position] // blocks).reshape((-1,) + (1,) * (len(dims) - 1 - position))
    return gain


def ranked_wide(own_key, dims, amount, skew):
    portions = [min(1 << octave, amount + 1 - (1 << octave)) * (1 << 20) // math.isqrt((1 << octave) ** skew) + 1 for octave in range((amount + 1).bit_length()) if 1 << octave <= amount]
    deviation = 1 + sum(portions) // (1 << 30)
    grid = np.cumsum(np.array([max(1, weight // deviation) for weight in portions]))
    pick = jax.random.randint(jax.random.fold_in(own_key, 1), dims, 0, int(grid[len(portions) - 1]))
    start = jnp.left_shift(1, jnp.searchsorted(jnp.asarray(grid, jnp.int32), pick, side="right").astype(jnp.int32))
    grade = start - 1 + jax.random.randint(jax.random.fold_in(own_key, 4), dims, 0, 1 << 30) % jnp.minimum(start, amount + 1 - start)
    return jax.random.permutation(jax.random.fold_in(own_key, 2), amount)[grade].astype(jnp.int32)


def centred(rng, extent, deviation, reach, cuts=(), kind=jnp.bfloat16):
    values = jax.random.normal(rng, extent, jnp.float32) * deviation
    if len(cuts) > 0:
        values = block_scale(rng, extent, cuts, -0.22, 0.18) * values
    return jnp.clip(values, min=-reach, max=reach).astype(kind)


def setup_inputs(seed: int = 0) -> dict:
    key_of = jax.random.split(jax.random.key(seed), 8)
    return {
        "layer_inputs": centred(key_of[0], (LAYERS, TOKENS, D), 1.0, 6.0, ((0, 8), (1, 32))),
        "output_grads": centred(key_of[1], (LAYERS, TOKENS, FF), 1.0, 6.0, ((0, 8), (1, 32))),
        "left_factors": centred(key_of[2], (LAYERS, QUERIES, RANK, FF), FF ** -0.5, 0.0546875, ((0, 8), (1, 32))),
        "right_factors": centred(key_of[3], (LAYERS, QUERIES, RANK, D), D ** -0.5, 0.078125, ((0, 8), (1, 32))),
        "strengths": jnp.clip(jnp.exp(math.log(4.0) - 2.7725887 * jax.random.uniform(key_of[4], (LAYERS, QUERIES, RANK), jnp.float32) ** block_scale(key_of[4], (LAYERS, QUERIES, RANK), ((0, 8), (1, 32)), -0.2, 0.2)), 0.25, 4.0).astype(jnp.bfloat16),
        "train_ids": place_ends(ranked_wide(key_of[5], (TOKENS,), VOCAB, 2), jax.random.fold_in(key_of[5], 3), 0, VOCAB - 1).astype(jnp.int32),
        "query_ids": place_ends(ranked_wide(key_of[6], (QUERIES, QLEN), VOCAB, 2), jax.random.fold_in(key_of[6], 3), 0, VOCAB - 1).astype(jnp.int32),
    }


def reference(layer_inputs, output_grads, left_factors, right_factors, strengths, train_ids, query_ids):
    query_count = left_factors.shape[1]
    rank_count = left_factors.shape[2]
    scaling = 1.0 / math.sqrt(rank_count * LAYERS)

    def one_layer(totals, stacked):
        inputs_now, grads_now, left_now, right_now, strength_now = stacked
        grad_proj = jnp.dot(grads_now, left_now.reshape(query_count * rank_count, -1).T, preferred_element_type=jnp.float32)
        input_proj = jnp.dot(inputs_now, right_now.reshape(query_count * rank_count, -1).T, preferred_element_type=jnp.float32)
        weighted = grad_proj * input_proj * strength_now.reshape(1, query_count * rank_count).astype(jnp.float32)
        layer_scores = weighted.reshape(-1, query_count, rank_count).sum(axis=2).T
        return (totals + layer_scores * scaling, None)
    starting = jnp.zeros((query_count, layer_inputs.shape[1]), jnp.float32)
    token_scores, unused = lax.scan(one_layer, starting, (layer_inputs, output_grads, left_factors, right_factors, strengths))
    matches = jnp.any(query_ids[:, :, None] == train_ids[None, None, :], axis=1).astype(token_scores.dtype)
    masked = token_scores * matches
    intersection = masked.reshape(query_count, -1, SEQ_LEN).sum(axis=2) * (1.0 / math.sqrt(SEQ_LEN))
    return (token_scores, intersection)
```

```python
import math

import jax
import jax.numpy as jnp
from jax import lax
from jax.sharding import Mesh, PartitionSpec as P

SEQ_LEN = 2048
NZ, NY, NC = 4, 4, 2
RING = ("z", "y", "c")


def ring_pairs(along_z):
    pairs = []
    for z in range(NZ):
        for y in range(NY):
            for c in range(NC):
                step = 1 - 2 * c
                to_z = (z + step) % NZ if along_z else z
                to_y = y if along_z else (y + step) % NY
                pairs.append(((z * NY + y) * NC + c, (to_z * NY + to_y) * NC + c))
    return pairs


def hop_y(x):
    return lax.ppermute(x, RING, ring_pairs(False))


def hop_z(x):
    return lax.ppermute(x, RING, ring_pairs(True))


def ring(x, hop, count):
    blocks = [x]
    for _ in range(count - 1):
        blocks.append(hop(blocks[-1]))
    return blocks


def swap(x):
    return lax.ppermute(x, "c", [(0, 1), (1, 0)])


def dot(factors, source):
    return lax.dot_general(
        factors, source, (((1,), (1,)), ((), ())), preferred_element_type=jnp.float32
    )


def local(layer_inputs, output_grads, left_factors, right_factors, strengths, train_ids, query_ids):
    acts, grads = layer_inputs[0], output_grads[0]
    left, right = left_factors[0, 0], right_factors[0, 0]
    rank, width = right.shape
    tokens = acts.shape[0]
    layers = lax.axis_size("layer")
    queries = query_ids.shape[0]
    z0, y0, c0 = lax.axis_index("z"), lax.axis_index("y"), lax.axis_index("c")
    layer_index = lax.axis_index("layer")

    right = jnp.concatenate(
        [right, jnp.broadcast_to(strengths[0, 0][:, None], (rank, 128))], axis=1
    )
    other_acts, other_grads = swap(acts), swap(grads)
    other_ids = swap(train_ids)

    right_y = ring(right, hop_y, NY)
    left_z = ring(left, hop_z, NZ)
    left_zy = [ring(block, hop_y, NY) for block in left_z]
    right_z = ring(jnp.concatenate(right_y, axis=0), hop_z, NZ)

    parts = []
    for i in range(NZ):
        left_rows = jnp.concatenate(left_zy[i], axis=0)
        right_rows = right_z[i][:, :width]
        weight = right_z[i][:, width : width + 1].astype(jnp.float32)
        halves = [
            dot(left_rows, g) * dot(right_rows, a) * weight
            for g, a in ((grads, acts), (other_grads, other_acts))
        ]
        both = jnp.concatenate(halves, axis=1)
        parts.append(both.reshape(NY, rank, 2 * tokens).sum(axis=1))
    scores = jnp.stack(parts) * (1.0 / math.sqrt(rank * layers))
    sign = 1 - 2 * c0
    zs, ys = jnp.arange(NZ), jnp.arange(NY)
    pick_z = (z0 - sign * zs) % NZ == zs[:, None]
    pick_y = (y0 - sign * ys) % NY == ys[:, None]
    scores = jnp.where(pick_z[:, :, None, None], scores[None], 0.0).sum(axis=1)
    scores = jnp.where(pick_y[None, :, :, None], scores[:, None], 0.0).sum(axis=2)
    scores = scores.reshape(layers, 2, 2, tokens)
    scores = jnp.where(c0 == 0, scores, scores[:, :, ::-1])
    sent = scores.transpose(0, 2, 1, 3).reshape(layers * NC, 2, tokens)
    got = lax.all_to_all(sent, ("layer", "c"), 0, 0, tiled=True)
    own_scores = got.reshape(layers, NC, 2, tokens).sum(axis=0)
    own_scores = own_scores.transpose(1, 0, 2).reshape(2 * NC, tokens)

    own_rows = queries // layers
    own_ids = lax.dynamic_slice_in_dim(query_ids, layer_index * own_rows, own_rows, 0)
    matches = jnp.any(own_ids[:, :, None] == train_ids[None, None, :], axis=1).astype(jnp.float32)
    seq_part = jnp.sum(own_scores * matches, axis=1) * (1.0 / math.sqrt(SEQ_LEN))
    sums = jnp.broadcast_to(seq_part[None, :, None], (NZ * NY * NC, own_rows, 128))
    sums = lax.all_to_all(sums, RING, 0, 0, tiled=True)[:, :, 0]
    intersection = sums.reshape(NZ, NY * NC, own_rows).sum(axis=1).T
    return (own_scores, intersection)


def solution(mesh):
    cut = Mesh(mesh.devices.reshape(-1, NZ, NY, NC), ("layer",) + RING)
    return jax.shard_map(
        local,
        mesh=cut,
        in_specs=(
            P("layer", RING, None),
            P("layer", RING, None),
            P("layer", RING, None, None),
            P("layer", RING, None, None),
            P("layer", RING, None),
            P(RING),
            P(),
        ),
        out_specs=(P("layer", RING), P("layer", None)),
        check_vma=False,
    )
```

```python
import math

import jax
import jax.numpy as jnp
from jax import lax
from jax.experimental import pallas as pl
from jax.experimental.pallas import tpu as pltpu
from jax.sharding import Mesh, PartitionSpec as P

SEQ_LEN = 2048
NZ, NY, NC = 4, 4, 2
RING = ("z", "y", "c")
VMEM = 12 << 20
PLAN = (
    "y01", "ga", "p1", "z1", "y02", "gg", "p3", "p2", "z2", "y12", "y03", "z3", "y21", "y31",
    "b1", "y23", "y32", "y22", "y11", "y13", "y33", "C0", "b2", "b3", "C1",
)
STEPS = (0, 1, -1, 2)


SOURCE = ("", "0", "0", "1")
WAY = (0, 1, -1, 1)


def pairs(along_z, way):
    out = []
    for z in range(NZ):
        for y in range(NY):
            for c in range(NC):
                step = way * (1 - 2 * c)
                to_z = (z + step) % NZ if along_z else z
                to_y = y if along_z else (y + step) % NY
                out.append(((z * NY + y) * NC + c, (to_z * NY + to_y) * NC + c))
    return out


def hop(x, along_z, way):
    return lax.ppermute(x, RING, pairs(along_z, way))


def swap(x):
    return lax.ppermute(x, "c", [(0, 1), (1, 0)])


def pack(right, strengths):
    rank, width = right.shape

    def kernel(right_ref, strength_ref, short_ref):
        short_ref[:, :width] = right_ref[...]
        row = jnp.broadcast_to(strength_ref[...].astype(jnp.float32), (rank, rank))
        eye = lax.broadcasted_iota(jnp.int32, (rank, rank), 0) == lax.broadcasted_iota(
            jnp.int32, (rank, rank), 1
        )
        column = jnp.sum(jnp.where(eye, row, 0.0), axis=1, keepdims=True)
        short_ref[:, width:] = jnp.broadcast_to(column, (rank, 128)).astype(right.dtype)

    return pl.pallas_call(
        kernel,
        out_shape=jax.ShapeDtypeStruct((rank, width + 128), right.dtype),
        name="pack",
    )(right, strengths)


def grad_part(blocks, sources):
    tokens, depth = sources[0].shape
    rows = sum(x.shape[0] for x in blocks)
    step = depth // 9

    def kernel(*refs):
        block_refs, rest = refs[: len(blocks)], refs[len(blocks) :]
        for s, out_ref in enumerate(rest[len(sources) :]):
            total = None
            for k in range(0, depth, step):
                factors = jnp.concatenate([r[:, k : k + step] for r in block_refs], axis=0)
                part = contract(rest[s][:, k : k + step], factors)
                total = part if total is None else total + part
            out_ref[...] = total

    return pl.pallas_call(
        kernel,
        out_shape=(jax.ShapeDtypeStruct((tokens, rows), jnp.float32),) * len(sources),
        name="grad_part",
        compiler_params=pltpu.CompilerParams(vmem_limit_bytes=VMEM),
    )(*blocks, *sources)


def score_part(bundles, sources, grad_parts, rank):
    tokens, depth = sources[0].shape
    rows = sum(x.shape[0] for x in bundles)
    step = depth // 4

    def kernel(*refs):
        bundle_refs, rest = refs[: len(bundles)], refs[len(bundles) : -1]
        out_ref = refs[-1]
        weight = jnp.concatenate([r[:, depth:] for r in bundle_refs], axis=0)
        weight = weight.astype(jnp.float32)[:, :1]
        for s in range(len(sources)):
            total = None
            for k in range(0, depth, step):
                factors = jnp.concatenate([r[:, k : k + step] for r in bundle_refs], axis=0)
                part = contract(rest[s][:, k : k + step], factors)
                total = part if total is None else total + part
            weighted = (total * rest[len(sources) + s][...]).T * weight
            mine = slice(s * tokens, (s + 1) * tokens)
            out_ref[:, mine] = weighted.reshape(rows // rank, rank, tokens).sum(axis=1)

    return pl.pallas_call(
        kernel,
        out_shape=jax.ShapeDtypeStruct((rows // rank, len(sources) * tokens), jnp.float32),
        name="score_part",
        compiler_params=pltpu.CompilerParams(vmem_limit_bytes=VMEM),
    )(*bundles, *sources, *grad_parts)


def contract(a, b):
    return lax.dot_general(a, b, (((1,), (1,)), ((), ())), preferred_element_type=jnp.float32)


def local(layer_inputs, output_grads, left_factors, right_factors, strengths, train_ids, query_ids):
    acts, grads = layer_inputs[0], output_grads[0]
    rank, high = left_factors.shape[2:]
    tokens = acts.shape[0]
    layers = lax.axis_size("layer")
    queries = query_ids.shape[0]
    z0, y0, c0 = lax.axis_index("z"), lax.axis_index("y"), lax.axis_index("c")
    layer_index = lax.axis_index("layer")

    long, short = left_factors[0, 0], pack(right_factors[0, 0], strengths[0])
    held = {"z0": long, "p0": short, "y00": long}
    last = None

    def start(task):
        if task[0] == "g":
            return swap(acts if task == "ga" else grads)
        count = int(task[-1])
        from_task = task[:-1] + SOURCE[count]
        if from_task not in held and task[0] == "b":
            held["b0"] = jnp.concatenate([held[f"p{j}"] for j in range(NY)], axis=0)
        return hop(held[from_task], task[0] in "zb", WAY[count])

    def compute(task):
        if task == "C0":
            blocks = [held[f"y{i}{j}"] for i in range(NZ) for j in range(NY)]
            return grad_part(blocks, [grads, held["gg"]])
        bundles = [held[f"b{i}"] for i in range(NZ)]
        return score_part(bundles, [acts, held["ga"]], held["C0"], rank)

    def after(x):
        return x if last is None else lax.optimization_barrier((x, last))[0]

    for task in PLAN:
        held[task] = last = compute(task) if task[0] == "C" else after(start(task))
        if task[0] == "z":
            held[f"y{task[1]}0"] = last
    scores = held["C1"].reshape(NZ, NY, -1)

    steps = jnp.array(STEPS, jnp.int32)
    way = 1 - 2 * c0
    pick_z = (z0 - way * steps) % NZ == jnp.arange(NZ)[:, None]
    pick_y = (y0 - way * steps) % NY == jnp.arange(NY)[:, None]
    scores = jnp.where(pick_z[:, :, None, None], scores[None], 0.0).sum(axis=1)
    scores = jnp.where(pick_y[None, :, :, None], scores[:, None], 0.0).sum(axis=2)
    scores = scores.reshape(layers, 2, NC, tokens) * (1.0 / math.sqrt(rank * layers))
    scores = jnp.where(c0 == 0, scores, scores[:, :, ::-1])
    sent = scores.transpose(0, 2, 1, 3).reshape(layers * NC, 2, tokens)
    got = lax.all_to_all(sent, ("layer", "c"), 0, 0, tiled=True)
    own_scores = got.reshape(layers, NC, 2, tokens).sum(axis=0)
    own_scores = own_scores.transpose(1, 0, 2).reshape(2 * NC, tokens)

    own_rows = queries // layers
    own_ids = lax.dynamic_slice_in_dim(query_ids, layer_index * own_rows, own_rows, 0)
    matches = jnp.any(own_ids[:, :, None] == train_ids[None, None, :], axis=1).astype(jnp.float32)
    seq_part = jnp.sum(own_scores * matches, axis=1) * (1.0 / math.sqrt(SEQ_LEN))
    sums = jnp.broadcast_to(seq_part[None, :, None], (NZ * NY * NC, own_rows, 128))
    sums = lax.all_to_all(sums, RING, 0, 0, tiled=True)[:, :, 0]
    intersection = sums.reshape(NZ, NY * NC, own_rows).sum(axis=1).T
    return (own_scores, intersection)


def solution(mesh):
    cut = Mesh(mesh.devices.reshape(-1, NZ, NY, NC), ("layer",) + RING)
    return jax.shard_map(
        local,
        mesh=cut,
        in_specs=(
            P("layer", RING, None),
            P("layer", RING, None),
            P("layer", RING, None, None),
            P("layer", RING, None, None),
            P("layer", RING, None),
            P(RING),
            P(),
        ),
        out_specs=(P("layer", RING), P("layer", None)),
        check_vma=False,
    )
```

```python
import math

import jax
import jax.numpy as jnp
from jax import lax
from jax.experimental import pallas as pl
from jax.experimental.pallas import tpu as pltpu
from jax.sharding import Mesh, PartitionSpec as P

SEQ_LEN = 2048
NZ, NY, NC = 4, 4, 2
RING = ("z", "y", "c")
VMEM = 12 << 20
PLAN = (
    "y01", "ga", "p1", "z1", "y02", "gg", "p3", "p2", "z2", "y12", "y03", "z3", "y21", "y31",
    "b1", "y23", "y32", "y22", "y11", "y13", "y33", "C0", "b2", "b3", "C1",
)
STEPS = (0, 1, -1, 2)


SOURCE = ("", "0", "0", "1")
WAY = (0, 1, -1, 1)


def pairs(along_z, way):
    out = []
    for z in range(NZ):
        for y in range(NY):
            for c in range(NC):
                step = way * (1 - 2 * c)
                to_z = (z + step) % NZ if along_z else z
                to_y = y if along_z else (y + step) % NY
                out.append(((z * NY + y) * NC + c, (to_z * NY + to_y) * NC + c))
    return out


def hop(x, along_z, way):
    return lax.ppermute(x, RING, pairs(along_z, way))


def swap(x):
    return lax.ppermute(x, "c", [(0, 1), (1, 0)])


def pack(right, strengths):
    rank, width = right.shape

    def kernel(right_ref, strength_ref, short_ref):
        short_ref[:, :width] = right_ref[...]
        row = jnp.broadcast_to(strength_ref[...].astype(jnp.float32), (rank, rank))
        eye = lax.broadcasted_iota(jnp.int32, (rank, rank), 0) == lax.broadcasted_iota(
            jnp.int32, (rank, rank), 1
        )
        column = jnp.sum(jnp.where(eye, row, 0.0), axis=1, keepdims=True)
        short_ref[:, width:] = jnp.broadcast_to(column, (rank, 128)).astype(right.dtype)

    return pl.pallas_call(
        kernel,
        out_shape=jax.ShapeDtypeStruct((rank, width + 128), right.dtype),
        name="pack",
        compiler_params=pltpu.CompilerParams(vmem_limit_bytes=4 << 20),
    )(right, strengths)


def grad_part(blocks, sources):
    tokens, depth = sources[0].shape
    rows = sum(x.shape[0] for x in blocks)
    step = depth // 9

    def kernel(*refs):
        block_refs, rest = refs[: len(blocks)], refs[len(blocks) :]
        for s, out_ref in enumerate(rest[len(sources) :]):
            total = None
            for k in range(0, depth, step):
                factors = jnp.concatenate([r[:, k : k + step] for r in block_refs], axis=0)
                part = contract(rest[s][:, k : k + step], factors)
                total = part if total is None else total + part
            out_ref[...] = total

    return pl.pallas_call(
        kernel,
        out_shape=(jax.ShapeDtypeStruct((tokens, rows), jnp.float32),) * len(sources),
        name="grad_part",
        compiler_params=pltpu.CompilerParams(vmem_limit_bytes=VMEM),
    )(*blocks, *sources)


def score_part(bundles, sources, grad_parts, rank):
    tokens, depth = sources[0].shape
    rows = sum(x.shape[0] for x in bundles)
    step = depth // 4

    def kernel(*refs):
        bundle_refs, rest = refs[: len(bundles)], refs[len(bundles) : -1]
        out_ref = refs[-1]
        weight = jnp.concatenate([r[:, depth:] for r in bundle_refs], axis=0)
        weight = weight.astype(jnp.float32)[:, :1]
        for s in range(len(sources)):
            total = None
            for k in range(0, depth, step):
                factors = jnp.concatenate([r[:, k : k + step] for r in bundle_refs], axis=0)
                part = contract(rest[s][:, k : k + step], factors)
                total = part if total is None else total + part
            weighted = (total * rest[len(sources) + s][...]).T * weight
            mine = slice(s * tokens, (s + 1) * tokens)
            out_ref[:, mine] = weighted.reshape(rows // rank, rank, tokens).sum(axis=1)

    return pl.pallas_call(
        kernel,
        out_shape=jax.ShapeDtypeStruct((rows // rank, len(sources) * tokens), jnp.float32),
        name="score_part",
        compiler_params=pltpu.CompilerParams(vmem_limit_bytes=VMEM),
    )(*bundles, *sources, *grad_parts)


def contract(a, b):
    return lax.dot_general(a, b, (((1,), (1,)), ((), ())), preferred_element_type=jnp.float32)


def local(layer_inputs, output_grads, left_factors, right_factors, strengths, train_ids, query_ids):
    acts, grads = layer_inputs[0], output_grads[0]
    rank, high = left_factors.shape[2:]
    tokens = acts.shape[0]
    layers = lax.axis_size("layer")
    queries = query_ids.shape[0]
    z0, y0, c0 = lax.axis_index("z"), lax.axis_index("y"), lax.axis_index("c")
    layer_index = lax.axis_index("layer")

    places = (z0, y0, c0, layer_index)
    arrays = (left_factors[0, 0], right_factors[0, 0], strengths[0], acts, grads)
    arrays, places = lax.optimization_barrier((arrays, places))
    long, right, own_strengths, acts, grads = arrays
    short = pack(right, own_strengths)
    held = {"z0": long, "p0": short, "y00": long}
    last = None

    def start(task):
        if task[0] == "g":
            return swap(acts if task == "ga" else grads)
        count = int(task[-1])
        from_task = task[:-1] + SOURCE[count]
        if from_task not in held and task[0] == "b":
            held["b0"] = jnp.concatenate([held[f"p{j}"] for j in range(NY)], axis=0)
        return hop(held[from_task], task[0] in "zb", WAY[count])

    def compute(task):
        if task == "C0":
            blocks = [held[f"y{i}{j}"] for i in range(NZ) for j in range(NY)]
            return grad_part(blocks, [grads, held["gg"]])
        bundles = [held[f"b{i}"] for i in range(NZ)]
        return score_part(bundles, [acts, held["ga"]], held["C0"], rank)

    def after(x):
        return x if last is None else lax.optimization_barrier((x, last))[0]

    for task in PLAN:
        held[task] = last = compute(task) if task[0] == "C" else after(start(task))
        if task[0] == "z":
            held[f"y{task[1]}0"] = last
    scores, z0, y0, c0, layer_index = lax.optimization_barrier((held["C1"], *places))
    scores = scores.reshape(NZ, NY, -1)

    steps = jnp.array(STEPS, jnp.int32)
    way = 1 - 2 * c0
    pick_z = (z0 - way * steps) % NZ == jnp.arange(NZ)[:, None]
    pick_y = (y0 - way * steps) % NY == jnp.arange(NY)[:, None]
    scores = jnp.where(pick_z[:, :, None, None], scores[None], 0.0).sum(axis=1)
    scores = jnp.where(pick_y[None, :, :, None], scores[:, None], 0.0).sum(axis=2)
    scores = scores.reshape(layers, 2, NC, tokens) * (1.0 / math.sqrt(rank * layers))
    scores = jnp.where(c0 == 0, scores, scores[:, :, ::-1])
    sent = scores.transpose(0, 2, 1, 3).reshape(layers * NC, 2, tokens)
    got = lax.all_to_all(sent, ("layer", "c"), 0, 0, tiled=True)
    own_scores = got.reshape(layers, NC, 2, tokens).sum(axis=0)
    own_scores = own_scores.transpose(1, 0, 2).reshape(2 * NC, tokens)

    own_rows = queries // layers
    own_ids = lax.dynamic_slice_in_dim(query_ids, layer_index * own_rows, own_rows, 0)
    matches = jnp.any(own_ids[:, :, None] == train_ids[None, None, :], axis=1).astype(jnp.float32)
    seq_part = jnp.sum(own_scores * matches, axis=1) * (1.0 / math.sqrt(SEQ_LEN))
    sums = jnp.broadcast_to(seq_part[None, :, None], (NZ * NY * NC, own_rows, 128))
    sums = lax.all_to_all(sums, RING, 0, 0, tiled=True)[:, :, 0]
    intersection = sums.reshape(NZ, NY * NC, own_rows).sum(axis=1).T
    return (own_scores, intersection)


def solution(mesh):
    cut = Mesh(mesh.devices.reshape(-1, NZ, NY, NC), ("layer",) + RING)
    return jax.shard_map(
        local,
        mesh=cut,
        in_specs=(
            P("layer", RING, None),
            P("layer", RING, None),
            P("layer", RING, None, None),
            P("layer", RING, None, None),
            P("layer", RING, None),
            P(RING),
            P(),
        ),
        out_specs=(P("layer", RING), P("layer", None)),
        check_vma=False,
    )
```

```python
import math

import jax
import jax.numpy as jnp
from jax import lax
from jax.experimental import pallas as pl
from jax.experimental.pallas import tpu as pltpu
from jax.sharding import Mesh, PartitionSpec as P

SEQ_LEN = 2048
NZ, NY, NC = 4, 4, 2
RING = ("z", "y", "c")
VMEM = 12 << 20
PLAN = (
    "y01", "ga", "p1", "z1", "y02", "gg", "p3", "p2", "z2", "y12", "y03", "z3", "y21", "y31",
    "b1", "y23", "y32", "y22", "y11", "C0", "y13", "y33", "C1", "b2", "b3", "C2",
)
BLOCKS = tuple(f"y{i}{j}" for i in range(NZ) for j in range(NY))
LATE = ("y13", "y33")
STEPS = (0, 1, -1, 2)


SOURCE = ("", "0", "0", "1")
WAY = (0, 1, -1, 1)


def pairs(along_z, way):
    out = []
    for z in range(NZ):
        for y in range(NY):
            for c in range(NC):
                step = way * (1 - 2 * c)
                to_z = (z + step) % NZ if along_z else z
                to_y = y if along_z else (y + step) % NY
                out.append(((z * NY + y) * NC + c, (to_z * NY + to_y) * NC + c))
    return out


def hop(x, along_z, way):
    return lax.ppermute(x, RING, pairs(along_z, way))


def swap(x):
    return lax.ppermute(x, "c", [(0, 1), (1, 0)])


def pack(right, strengths):
    rank, width = right.shape

    def kernel(right_ref, strength_ref, short_ref):
        short_ref[:, :width] = right_ref[...]
        row = jnp.broadcast_to(strength_ref[...].astype(jnp.float32), (rank, rank))
        eye = lax.broadcasted_iota(jnp.int32, (rank, rank), 0) == lax.broadcasted_iota(
            jnp.int32, (rank, rank), 1
        )
        column = jnp.sum(jnp.where(eye, row, 0.0), axis=1, keepdims=True)
        short_ref[:, width:] = jnp.broadcast_to(column, (rank, 128)).astype(right.dtype)

    return pl.pallas_call(
        kernel,
        out_shape=jax.ShapeDtypeStruct((rank, width + 128), right.dtype),
        name="pack",
        compiler_params=pltpu.CompilerParams(vmem_limit_bytes=4 << 20),
    )(right, strengths)


def grad_part(blocks, sources):
    tokens, depth = sources[0].shape
    rows = sum(x.shape[0] for x in blocks)
    step = depth // 9

    def kernel(*refs):
        block_refs, rest = refs[: len(blocks)], refs[len(blocks) :]
        for s, out_ref in enumerate(rest[len(sources) :]):
            total = None
            for k in range(0, depth, step):
                factors = jnp.concatenate([r[:, k : k + step] for r in block_refs], axis=0)
                part = contract(factors, rest[s][:, k : k + step])
                total = part if total is None else total + part
            out_ref[...] = total

    return pl.pallas_call(
        kernel,
        out_shape=(jax.ShapeDtypeStruct((rows, tokens), jnp.float32),) * len(sources),
        name="grad_part",
        compiler_params=pltpu.CompilerParams(vmem_limit_bytes=VMEM),
        cost_estimate=pl.CostEstimate(
            flops=1, bytes_accessed=1, transcendentals=0
        ),
    )(*blocks, *sources)


def score_part(bundles, sources, early, late, rank):
    tokens, depth = sources[0].shape
    rows = sum(x.shape[0] for x in bundles)
    step = depth // 4
    count = len(sources)

    def kernel(*refs):
        bundle_refs, rest = refs[: len(bundles)], refs[len(bundles) : -1]
        out_ref = refs[-1]
        weight = jnp.concatenate([r[:, depth:] for r in bundle_refs], axis=0)
        weight = weight.astype(jnp.float32)[:, :1]
        for s in range(count):
            total = None
            for k in range(0, depth, step):
                factors = jnp.concatenate([r[:, k : k + step] for r in bundle_refs], axis=0)
                part = contract(factors, rest[s][:, k : k + step])
                total = part if total is None else total + part
            early_ref, late_ref = rest[count + s], rest[2 * count + s]
            pieces, e, l = [], 0, 0
            for key in BLOCKS:
                if key in LATE:
                    pieces.append(late_ref[l : l + rank, :])
                    l += rank
                else:
                    pieces.append(early_ref[e : e + rank, :])
                    e += rank
            weighted = total * jnp.concatenate(pieces, axis=0) * weight
            mine = slice(s * tokens, (s + 1) * tokens)
            out_ref[:, mine] = weighted.reshape(rows // rank, rank, tokens).sum(axis=1)

    return pl.pallas_call(
        kernel,
        out_shape=jax.ShapeDtypeStruct((rows // rank, count * tokens), jnp.float32),
        name="score_part",
        compiler_params=pltpu.CompilerParams(vmem_limit_bytes=VMEM),
    )(*bundles, *sources, *early, *late)


def contract(a, b):
    return lax.dot_general(a, b, (((1,), (1,)), ((), ())), preferred_element_type=jnp.float32)


def local(layer_inputs, output_grads, left_factors, right_factors, strengths, train_ids, query_ids):
    acts, grads = layer_inputs[0], output_grads[0]
    rank, high = left_factors.shape[2:]
    tokens = acts.shape[0]
    layers = lax.axis_size("layer")
    queries = query_ids.shape[0]
    z0, y0, c0 = lax.axis_index("z"), lax.axis_index("y"), lax.axis_index("c")
    layer_index = lax.axis_index("layer")

    places = (z0, y0, c0, layer_index)
    arrays = (left_factors[0, 0], right_factors[0, 0], strengths[0], acts, grads)
    arrays, places = lax.optimization_barrier((arrays, places))
    long, right, own_strengths, acts, grads = arrays
    short = pack(right, own_strengths)
    held = {"z0": long, "p0": short, "y00": long}
    last = None

    def start(task):
        if task[0] == "g":
            return swap(acts if task == "ga" else grads)
        count = int(task[-1])
        from_task = task[:-1] + SOURCE[count]
        if from_task not in held and task[0] == "b":
            held["b0"] = jnp.concatenate([held[f"p{j}"] for j in range(NY)], axis=0)
        return hop(held[from_task], task[0] in "zb", WAY[count])

    def compute(task):
        if task == "C2":
            bundles = [held[f"b{i}"] for i in range(NZ)]
            return score_part(bundles, [acts, held["ga"]], held["C0"], held["C1"], rank)
        blocks = [held[key] for key in BLOCKS if (key in LATE) == (task == "C1")]
        blocks[0] = after(blocks[0])
        return grad_part(blocks, [grads, held["gg"]])

    def after(x):
        return x if last is None else lax.optimization_barrier((x, last))[0]

    for task in PLAN:
        held[task] = last = compute(task) if task[0] == "C" else after(start(task))
        if task[0] == "z":
            held[f"y{task[1]}0"] = last
    scores, z0, y0, c0, layer_index = lax.optimization_barrier((held["C2"], *places))
    scores = scores.reshape(NZ, NY, -1)

    steps = jnp.array(STEPS, jnp.int32)
    way = 1 - 2 * c0
    pick_z = (z0 - way * steps) % NZ == jnp.arange(NZ)[:, None]
    pick_y = (y0 - way * steps) % NY == jnp.arange(NY)[:, None]
    scores = jnp.where(pick_z[:, :, None, None], scores[None], 0.0).sum(axis=1)
    scores = jnp.where(pick_y[None, :, :, None], scores[:, None], 0.0).sum(axis=2)
    scores = scores.reshape(layers, 2, NC, tokens) * (1.0 / math.sqrt(rank * layers))
    scores = jnp.where(c0 == 0, scores, scores[:, :, ::-1])
    sent = scores.transpose(0, 2, 1, 3).reshape(layers * NC, 2, tokens)
    got = lax.all_to_all(sent, ("layer", "c"), 0, 0, tiled=True)
    own_scores = got.reshape(layers, NC, 2, tokens).sum(axis=0)
    own_scores = own_scores.transpose(1, 0, 2).reshape(2 * NC, tokens)

    own_rows = queries // layers
    own_ids = lax.dynamic_slice_in_dim(query_ids, layer_index * own_rows, own_rows, 0)
    matches = jnp.any(own_ids[:, :, None] == train_ids[None, None, :], axis=1).astype(jnp.float32)
    seq_part = jnp.sum(own_scores * matches, axis=1) * (1.0 / math.sqrt(SEQ_LEN))
    sums = jnp.broadcast_to(seq_part[None, :, None], (NZ * NY * NC, own_rows, 128))
    sums = lax.all_to_all(sums, RING, 0, 0, tiled=True)[:, :, 0]
    intersection = sums.reshape(NZ, NY * NC, own_rows).sum(axis=1).T
    return (own_scores, intersection)


def solution(mesh):
    cut = Mesh(mesh.devices.reshape(-1, NZ, NY, NC), ("layer",) + RING)
    return jax.shard_map(
        local,
        mesh=cut,
        in_specs=(
            P("layer", RING, None),
            P("layer", RING, None),
            P("layer", RING, None, None),
            P("layer", RING, None, None),
            P("layer", RING, None),
            P(RING),
            P(),
        ),
        out_specs=(P("layer", RING), P("layer", None)),
        check_vma=False,
    )
```

```python
import math

import jax
import jax.numpy as jnp
from jax import lax
from jax.experimental import pallas as pl
from jax.experimental.pallas import tpu as pltpu
from jax.sharding import Mesh, PartitionSpec as P

SEQ_LEN = 2048
NZ, NY, NC = 4, 4, 2
RING = ("z", "y", "c")
VMEM = 12 << 20
PLAN = (
    "p1", "y01", "ga", "z1", "y02", "gg", "p3", "p2", "z2", "y12", "y03", "z3", "y21", "y31",
    "b1", "y23", "y32", "y22", "y11", "C0", "y13", "y33", "C1", "b2", "b3", "C2",
)
BLOCKS = tuple(f"y{i}{j}" for i in range(NZ) for j in range(NY))
LATE = ("y13", "y33")
STEPS = (0, 1, -1, 2)


SOURCE = ("", "0", "0", "1")
WAY = (0, 1, -1, 1)


def pairs(along_z, way):
    out = []
    for z in range(NZ):
        for y in range(NY):
            for c in range(NC):
                step = way * (1 - 2 * c)
                to_z = (z + step) % NZ if along_z else z
                to_y = y if along_z else (y + step) % NY
                out.append(((z * NY + y) * NC + c, (to_z * NY + to_y) * NC + c))
    return out


def hop(x, along_z, way):
    return lax.ppermute(x, RING, pairs(along_z, way))


def swap(x):
    return lax.ppermute(x, "c", [(0, 1), (1, 0)])


def pack(right, strengths):
    rank, width = right.shape

    def kernel(right_ref, strength_ref, short_ref):
        short_ref[:, :width] = right_ref[...]
        row = jnp.broadcast_to(strength_ref[...].astype(jnp.float32), (rank, rank))
        eye = lax.broadcasted_iota(jnp.int32, (rank, rank), 0) == lax.broadcasted_iota(
            jnp.int32, (rank, rank), 1
        )
        column = jnp.sum(jnp.where(eye, row, 0.0), axis=1, keepdims=True)
        short_ref[:, width:] = jnp.broadcast_to(column, (rank, 128)).astype(right.dtype)

    return pl.pallas_call(
        kernel,
        out_shape=jax.ShapeDtypeStruct((rank, width + 128), right.dtype),
        name="pack",
        compiler_params=pltpu.CompilerParams(vmem_limit_bytes=4 << 20),
    )(right, strengths)


def grad_part(blocks, sources):
    tokens, depth = sources[0].shape
    rows = sum(x.shape[0] for x in blocks)
    step = depth // 9

    def kernel(*refs):
        block_refs, rest = refs[: len(blocks)], refs[len(blocks) :]
        for s, out_ref in enumerate(rest[len(sources) :]):
            total = None
            for k in range(0, depth, step):
                factors = jnp.concatenate([r[:, k : k + step] for r in block_refs], axis=0)
                part = contract(factors, rest[s][:, k : k + step])
                total = part if total is None else total + part
            out_ref[...] = total

    return pl.pallas_call(
        kernel,
        out_shape=(jax.ShapeDtypeStruct((rows, tokens), jnp.float32),) * len(sources),
        name="grad_part",
        compiler_params=pltpu.CompilerParams(vmem_limit_bytes=VMEM),
        cost_estimate=pl.CostEstimate(
            flops=1, bytes_accessed=1, transcendentals=0
        ),
    )(*blocks, *sources)


def score_part(bundles, sources, early, late, rank):
    tokens, depth = sources[0].shape
    rows = sum(x.shape[0] for x in bundles)
    step = depth // 4
    count = len(sources)

    def kernel(*refs):
        bundle_refs, rest = refs[: len(bundles)], refs[len(bundles) : -1]
        out_ref = refs[-1]
        weight = jnp.concatenate([r[:, depth:] for r in bundle_refs], axis=0)
        weight = weight.astype(jnp.float32)[:, :1]
        for s in range(count):
            total = None
            for k in range(0, depth, step):
                factors = jnp.concatenate([r[:, k : k + step] for r in bundle_refs], axis=0)
                part = contract(factors, rest[s][:, k : k + step])
                total = part if total is None else total + part
            early_ref, late_ref = rest[count + s], rest[2 * count + s]
            pieces, e, l = [], 0, 0
            for key in BLOCKS:
                if key in LATE:
                    pieces.append(late_ref[l : l + rank, :])
                    l += rank
                else:
                    pieces.append(early_ref[e : e + rank, :])
                    e += rank
            weighted = total * jnp.concatenate(pieces, axis=0) * weight
            mine = slice(s * tokens, (s + 1) * tokens)
            out_ref[:, mine] = weighted.reshape(rows // rank, rank, tokens).sum(axis=1)

    return pl.pallas_call(
        kernel,
        out_shape=jax.ShapeDtypeStruct((rows // rank, count * tokens), jnp.float32),
        name="score_part",
        compiler_params=pltpu.CompilerParams(vmem_limit_bytes=VMEM),
    )(*bundles, *sources, *early, *late)


def contract(a, b):
    return lax.dot_general(a, b, (((1,), (1,)), ((), ())), preferred_element_type=jnp.float32)


def local(layer_inputs, output_grads, left_factors, right_factors, strengths, train_ids, query_ids):
    acts, grads = layer_inputs[0], output_grads[0]
    rank, high = left_factors.shape[2:]
    tokens = acts.shape[0]
    layers = lax.axis_size("layer")
    queries = query_ids.shape[0]
    z0, y0, c0 = lax.axis_index("z"), lax.axis_index("y"), lax.axis_index("c")
    layer_index = lax.axis_index("layer")

    places = (z0, y0, c0, layer_index)
    arrays = (left_factors[0, 0], right_factors[0, 0], strengths[0], acts, grads)
    arrays, places = lax.optimization_barrier((arrays, places))
    long, right, own_strengths, acts, grads = arrays
    short = pack(right, own_strengths)
    held = {"z0": long, "p0": short, "y00": long}
    last = None

    def start(task):
        if task[0] == "g":
            return swap(acts if task == "ga" else grads)
        count = int(task[-1])
        from_task = task[:-1] + SOURCE[count]
        if from_task not in held and task[0] == "b":
            held["b0"] = jnp.concatenate([held[f"p{j}"] for j in range(NY)], axis=0)
        return hop(held[from_task], task[0] in "zb", WAY[count])

    def compute(task):
        if task == "C2":
            bundles = [held[f"b{i}"] for i in range(NZ)]
            return score_part(bundles, [acts, held["ga"]], held["C0"], held["C1"], rank)
        blocks = [held[key] for key in BLOCKS if (key in LATE) == (task == "C1")]
        blocks[0] = after(blocks[0])
        return grad_part(blocks, [grads, held["gg"]])

    def after(x):
        return x if last is None else lax.optimization_barrier((x, last))[0]

    for task in PLAN:
        held[task] = last = compute(task) if task[0] == "C" else after(start(task))
        if task[0] == "z":
            held[f"y{task[1]}0"] = last
    scores, z0, y0, c0, layer_index = lax.optimization_barrier((held["C2"], *places))
    scores = scores.reshape(NZ, NY, -1)

    steps = jnp.array(STEPS, jnp.int32)
    way = 1 - 2 * c0
    pick_z = (z0 - way * steps) % NZ == jnp.arange(NZ)[:, None]
    pick_y = (y0 - way * steps) % NY == jnp.arange(NY)[:, None]
    scores = jnp.where(pick_z[:, :, None, None], scores[None], 0.0).sum(axis=1)
    scores = jnp.where(pick_y[None, :, :, None], scores[:, None], 0.0).sum(axis=2)
    scores = scores.reshape(layers, 2, NC, tokens) * (1.0 / math.sqrt(rank * layers))
    scores = jnp.where(c0 == 0, scores, scores[:, :, ::-1])
    sent = scores.transpose(0, 2, 1, 3).reshape(layers * NC, 2, tokens)
    got = lax.all_to_all(sent, ("layer", "c"), 0, 0, tiled=True)
    own_scores = got.reshape(layers, NC, 2, tokens).sum(axis=0)
    own_scores = own_scores.transpose(1, 0, 2).reshape(2 * NC, tokens)

    own_rows = queries // layers
    own_ids = lax.dynamic_slice_in_dim(query_ids, layer_index * own_rows, own_rows, 0)
    matches = jnp.any(own_ids[:, :, None] == train_ids[None, None, :], axis=1).astype(jnp.float32)
    seq_part = jnp.sum(own_scores * matches, axis=1) * (1.0 / math.sqrt(SEQ_LEN))
    sums = jnp.broadcast_to(seq_part[None, :, None], (NZ * NY * NC, own_rows, 128))
    sums = lax.all_to_all(sums, RING, 0, 0, tiled=True)[:, :, 0]
    intersection = sums.reshape(NZ, NY * NC, own_rows).sum(axis=1).T
    return (own_scores, intersection)


def solution(mesh):
    cut = Mesh(mesh.devices.reshape(-1, NZ, NY, NC), ("layer",) + RING)
    return jax.shard_map(
        local,
        mesh=cut,
        in_specs=(
            P("layer", RING, None),
            P("layer", RING, None),
            P("layer", RING, None, None),
            P("layer", RING, None, None),
            P("layer", RING, None),
            P(RING),
            P(),
        ),
        out_specs=(P("layer", RING), P("layer", None)),
        check_vma=False,
    )
```

```python
import math

import jax
import jax.numpy as jnp
from jax import lax
from jax.experimental import pallas as pl
from jax.experimental.pallas import tpu as pltpu
from jax.sharding import Mesh, PartitionSpec as P

SEQ_LEN = 2048
NZ, NY, NC = 4, 4, 2
RING = ("z", "y", "c")
VMEM = 12 << 20
PLAN = (
    "p1", "y01", "ga", "z1", "y02", "gg", "p3", "p2", "z2", "y12", "y03", "z3", "y21", "y31",
    "b1", "y23", "y32", "y22", "y11", "C0", "y13", "y33", "C1", "b2", "b3", "C2",
)
BLOCKS = tuple(f"y{i}{j}" for i in range(NZ) for j in range(NY))
LATE = ("y13", "y33")
STEPS = (0, 1, -1, 2)


SOURCE = ("", "0", "0", "1")
WAY = (0, 1, -1, 1)


def pairs(along_z, way):
    out = []
    for z in range(NZ):
        for y in range(NY):
            for c in range(NC):
                step = way * (1 - 2 * c)
                to_z = (z + step) % NZ if along_z else z
                to_y = y if along_z else (y + step) % NY
                out.append(((z * NY + y) * NC + c, (to_z * NY + to_y) * NC + c))
    return out


def hop(x, along_z, way):
    return lax.ppermute(x, RING, pairs(along_z, way))


def swap(x):
    return lax.ppermute(x, "c", [(0, 1), (1, 0)])


def pack(right, strengths):
    rank, width = right.shape

    def kernel(right_ref, strength_ref, short_ref):
        short_ref[:, :width] = right_ref[...]
        row = jnp.broadcast_to(strength_ref[...].astype(jnp.float32), (rank, rank))
        eye = lax.broadcasted_iota(jnp.int32, (rank, rank), 0) == lax.broadcasted_iota(
            jnp.int32, (rank, rank), 1
        )
        column = jnp.sum(jnp.where(eye, row, 0.0), axis=1, keepdims=True)
        short_ref[:, width:] = jnp.broadcast_to(column, (rank, 128)).astype(right.dtype)

    return pl.pallas_call(
        kernel,
        out_shape=jax.ShapeDtypeStruct((rank, width + 128), right.dtype),
        name="pack",
        compiler_params=pltpu.CompilerParams(vmem_limit_bytes=4 << 20),
    )(right, strengths)


def grad_part(blocks, sources):
    tokens, depth = sources[0].shape
    rows = sum(x.shape[0] for x in blocks)
    step = depth // 9

    def kernel(*refs):
        block_refs, rest = refs[: len(blocks)], refs[len(blocks) :]
        for s, out_ref in enumerate(rest[len(sources) :]):
            total = None
            for k in range(0, depth, step):
                factors = jnp.concatenate([r[:, k : k + step] for r in block_refs], axis=0)
                part = contract(factors, rest[s][:, k : k + step])
                total = part if total is None else total + part
            out_ref[...] = total

    return pl.pallas_call(
        kernel,
        out_shape=(jax.ShapeDtypeStruct((rows, tokens), jnp.float32),) * len(sources),
        name="grad_part",
        compiler_params=pltpu.CompilerParams(vmem_limit_bytes=VMEM),
        cost_estimate=pl.CostEstimate(
            flops=1, bytes_accessed=1, transcendentals=0
        ),
    )(*blocks, *sources)


def score_part(bundles, sources, early, late, rank):
    tokens, depth = sources[0].shape
    rows = sum(x.shape[0] for x in bundles)
    step = depth // 4
    count = len(sources)

    def kernel(*refs):
        bundle_refs, rest = refs[: len(bundles)], refs[len(bundles) : -1]
        out_ref = refs[-1]
        weight = jnp.concatenate([r[:, depth:] for r in bundle_refs], axis=0)
        weight = weight.astype(jnp.float32)[:, :1]
        for s in range(count):
            total = None
            for k in range(0, depth, step):
                factors = jnp.concatenate([r[:, k : k + step] for r in bundle_refs], axis=0)
                part = contract(factors, rest[s][:, k : k + step])
                total = part if total is None else total + part
            early_ref, late_ref = rest[count + s], rest[2 * count + s]
            pieces, e, l = [], 0, 0
            for key in BLOCKS:
                if key in LATE:
                    pieces.append(late_ref[l : l + rank, :])
                    l += rank
                else:
                    pieces.append(early_ref[e : e + rank, :])
                    e += rank
            weighted = total * jnp.concatenate(pieces, axis=0) * weight
            mine = slice(s * tokens, (s + 1) * tokens)
            out_ref[:, mine] = weighted.reshape(rows // rank, rank, tokens).sum(axis=1)

    return pl.pallas_call(
        kernel,
        out_shape=jax.ShapeDtypeStruct((rows // rank, count * tokens), jnp.float32),
        name="score_part",
        compiler_params=pltpu.CompilerParams(vmem_limit_bytes=VMEM),
    )(*bundles, *sources, *early, *late)


def contract(a, b):
    return lax.dot_general(a, b, (((1,), (1,)), ((), ())), preferred_element_type=jnp.float32)


def local(layer_inputs, output_grads, left_factors, right_factors, strengths, train_ids, query_ids):
    acts, grads = layer_inputs[0], output_grads[0]
    rank, high = left_factors.shape[2:]
    tokens = acts.shape[0]
    layers = lax.axis_size("layer")
    queries = query_ids.shape[0]
    z0, y0, c0 = lax.axis_index("z"), lax.axis_index("y"), lax.axis_index("c")
    layer_index = lax.axis_index("layer")

    places = (z0, y0, c0, layer_index)
    arrays = (left_factors[0, 0], right_factors[0, 0], strengths[0], acts, grads)
    arrays, places = lax.optimization_barrier((arrays, places))
    long, right, own_strengths, acts, grads = arrays
    short = pack(right, own_strengths)
    held = {"z0": long, "p0": short, "y00": long}
    last = None

    def start(task):
        if task[0] == "g":
            return swap(acts if task == "ga" else grads)
        count = int(task[-1])
        from_task = task[:-1] + SOURCE[count]
        if from_task not in held and task[0] == "b":
            held["b0"] = jnp.concatenate([held[f"p{j}"] for j in range(NY)], axis=0)
        return hop(held[from_task], task[0] in "zb", WAY[count])

    def compute(task):
        if task == "C2":
            bundles = [held[f"b{i}"] for i in range(NZ)]
            return score_part(bundles, [acts, held["ga"]], held["C0"], held["C1"], rank)
        blocks = [held[key] for key in BLOCKS if (key in LATE) == (task == "C1")]
        blocks[0] = after(blocks[0])
        return grad_part(blocks, [grads, held["gg"]])

    def after(x):
        return x if last is None else lax.optimization_barrier((x, last))[0]

    for task in PLAN:
        held[task] = last = compute(task) if task[0] == "C" else after(start(task))
        if task[0] == "z":
            held[f"y{task[1]}0"] = last
    scores, z0, y0, c0, layer_index = lax.optimization_barrier((held["C2"], *places))
    scores = scores.reshape(NZ, NY, -1)

    steps = jnp.array(STEPS, jnp.int32)
    way = 1 - 2 * c0
    pick_z = (z0 - way * steps) % NZ == jnp.arange(NZ)[:, None]
    pick_y = (y0 - way * steps) % NY == jnp.arange(NY)[:, None]
    scores = jnp.where(pick_z[:, :, None, None], scores[None], 0.0).sum(axis=1)
    scores = jnp.where(pick_y[None, :, :, None], scores[:, None], 0.0).sum(axis=2)
    scores = scores.reshape(layers, 2, NC, tokens) * (1.0 / math.sqrt(rank * layers))
    scores = jnp.where(c0 == 0, scores, scores[:, :, ::-1])
    sent = scores.transpose(0, 2, 1, 3).reshape(layers * NC, 2, tokens)
    got = lax.all_to_all(sent, ("layer", "c"), 0, 0, tiled=True)
    own_scores = got.reshape(layers, NC, 2, tokens).sum(axis=0)
    own_scores = own_scores.transpose(1, 0, 2).reshape(2 * NC, tokens)

    own_rows = queries // layers
    own_ids = lax.dynamic_slice_in_dim(query_ids, layer_index * own_rows, own_rows, 0)
    matches = jnp.any(own_ids[:, :, None] == train_ids[None, None, :], axis=1).astype(jnp.float32)
    seq_part = jnp.sum(own_scores * matches, axis=1) * (1.0 / math.sqrt(SEQ_LEN))
    sums = jnp.broadcast_to(seq_part[None, None, :], (NZ * NY * NC, 1, own_rows))
    sums = lax.all_to_all(sums, RING, 0, 0, tiled=True)[:, 0]
    intersection = sums.reshape(NZ, NY * NC, own_rows).sum(axis=1).T
    return (own_scores, intersection)


def solution(mesh):
    cut = Mesh(mesh.devices.reshape(-1, NZ, NY, NC), ("layer",) + RING)
    return jax.shard_map(
        local,
        mesh=cut,
        in_specs=(
            P("layer", RING, None),
            P("layer", RING, None),
            P("layer", RING, None, None),
            P("layer", RING, None, None),
            P("layer", RING, None),
            P(RING),
            P(),
        ),
        out_specs=(P("layer", RING), P("layer", None)),
        check_vma=False,
    )
```
